32 devices in a mesh: dp: 8 (over z, y), tensor: 4 (over x, core).
Axes of the slice: x: 2, y: 2, z: 4, core: 2. Of those that a mesh axis runs over, the one named last changes fastest.
Arguments:
- gate_act: bfloat16 [2048, 14336], P('dp', 'tensor'), may hold values from -6 to 6
- up_act: bfloat16 [2048, 14336], P('dp', 'tensor'), may hold values from -6 to 6
- out_grad: bfloat16 [2048, 4096], P(('dp', 'tensor')), may hold values from -6 to 6
- down_weight: bfloat16 [4096, 14336], P(None, 'tensor'), may hold values from -0.046875 to 0.046875
- master_weight: float32 [4096, 14336], P('dp', 'tensor'), may hold values from -0.046875 to 0.046875
- round_bits: int32 [4096, 14336], P('dp', 'tensor'), may hold values from 0 to 16383
Outputs:
- layer_out: bfloat16 [2048, 4096], P(('dp', 'tensor'))
- gate_grad: bfloat16 [2048, 14336], P('dp', 'tensor')
- up_grad: bfloat16 [2048, 14336], P('dp', 'tensor')
- new_master: float32 [4096, 14336], P('dp', 'tensor')
- new_weight: bfloat16 [4096, 14336], P('dp', 'tensor')
The draws below stay inside these ranges and needn't reach their ends.
All inputs are finite; a program needn't handle non-finite values.
Results may differ from the reference program's by a relative error of at most 0.0012.
The reference program's roundings to bfloat16 on the way (of `hidden`) count: a program that leaves them out, or rounds other values in their place, can miss the bound.
Values may be sent and summed in bfloat16 or wider, within the bound.
A program may use at most 128 MiB of HBM per device.

```python
import jax
import jax.numpy as jnp
from jax import lax

D = 4096
FF = 14336
TOKENS = 2048


def plant(array, stream_key, smallest, high):
    dims = array.shape
    spot = [jax.random.randint(jax.random.fold_in(stream_key, axis), (), 0, dims[axis]) for axis in range(len(dims))]
    array = array.at[tuple(spot)].set(smallest)
    longest = dims.index(max(dims))
    spot[longest] = (spot[longest] + 1) % dims[longest]
    return array.at[tuple(spot)].set(high)


def with_spikes(result, own_key, source, target, parts, factor):
    def block_of(dim):
        return (jnp.arange(result.shape[dim]) // (result.shape[dim] // parts)).reshape((-1,) + (1,) * (result.ndim - 1 - dim))

    one_side = jax.random.permutation(own_key, parts)[block_of(target)]
    second = (block_of(target) + parts // 2) % parts
    return jnp.where((block_of(source) == one_side) | (block_of(source) == second), factor * result, result)


def level_of(stream_key, extent, shards, least, high):
    factor_of, own = 1.0, jax.random.fold_in(stream_key, 6)
    for axis_at, parts in shards:
        steps = jnp.exp(jax.random.uniform(jax.random.fold_in(own, axis_at), (parts,), jnp.float32, least / len(shards), high / len(shards)))
        factor_of = factor_of * jnp.repeat(steps, extent[axis_at] // parts).reshape([-1 if axis == axis_at else 1 for axis in range(len(extent))])
    return factor_of


def scatter_about(stream_key, extent, deviation, most, split=(), held_as=jnp.bfloat16):
    values = deviation * jax.random.normal(stream_key, extent, jnp.float32)
    if split:
        values = values * level_of(stream_key, extent, split, -0.22, 0.18)
    return jnp.clip(values, -most, most).astype(held_as)


def gaussian_with(own_key, shape, spread, limit, shards, heavy, held_as=jnp.bfloat16):
    drawn = spread * jax.random.normal(own_key, shape, jnp.float32)
    if shards:
        drawn = drawn * level_of(own_key, shape, shards, -0.22, 0.18)
    return jnp.clip(with_spikes(drawn, jax.random.fold_in(own_key, 3), *heavy), -limit, limit).astype(held_as)


def setup_inputs(seed: int = 0) -> dict:
    streams_of = jax.random.split(jax.random.key(seed), 7)
    return {
        "gate_act": scatter_about(streams_of[0], (TOKENS, FF), 1.0, 6.0, ((0, 8), (1, 4))),
        "up_act": scatter_about(streams_of[1], (TOKENS, FF), 1.0, 6.0, ((0, 8), (1, 4))),
        "out_grad": gaussian_with(streams_of[2], (TOKENS, D), 1.0, 6.0, ((0, 32),), (0, 1, 32, 2.75)),
        "down_weight": scatter_about(streams_of[3], (D, FF), FF ** -0.5, 0.046875, ((1, 4),)),
        "master_weight": scatter_about(streams_of[4], (D, FF), FF ** -0.5, 0.046875, ((0, 8), (1, 4)), jnp.float32),
        "round_bits": plant(jax.random.randint(streams_of[5], (D, FF), 0, 16384), jax.random.fold_in(streams_of[5], 1), 0, 16383).astype(jnp.int32),
    }


learn_rate = 0.5
dither_scale = 1.0 / 64.0


def reference(gate_act, up_act, out_grad, down_weight, master_weight, round_bits):
    g = gate_act.astype(jnp.float32)
    u = up_act.astype(jnp.float32)
    sig = jax.nn.sigmoid(g)
    act = g * sig
    hidden = (act * u).astype(jnp.bfloat16)
    layer_out = lax.dot_general(hidden, down_weight, (((1,), (1,)), ((), ())),
                                preferred_element_type=jnp.float32).astype(jnp.bfloat16)
    hidden_grad = jnp.dot(out_grad, down_weight, preferred_element_type=jnp.float32)
    up_grad = (hidden_grad * act).astype(jnp.bfloat16)
    gate_grad = (hidden_grad * u * sig * (1.0 + g * (1.0 - sig))).astype(jnp.bfloat16)
    weight_grad = lax.dot_general(out_grad, hidden, (((0,), (0,)), ((), ())),
                                  preferred_element_type=jnp.float32)
    new_master = master_weight - learn_rate * (weight_grad / TOKENS)
    dither = (round_bits.astype(jnp.float32) + 0.5) / 16384.0
    new_weight = (new_master + (dither - 0.5) * jnp.abs(new_master) * dither_scale).astype(jnp.bfloat16)
    return layer_out, gate_grad, up_grad, new_master, new_weight
```

```python
import functools

import jax
import jax.numpy as jnp
from jax import lax
from jax.experimental import pallas as pl
from jax.experimental.pallas import tpu as pltpu
from jax.sharding import PartitionSpec as P

learn_rate = 0.5
dither_scale = 1.0 / 64.0


def arrivals(lines):
    return [
        [
            (way, hops)
            for hops in range(1, lines)
            for way, good in ((1, z >= hops), (-1, z + hops < lines))
            if good
        ]
        for z in range(lines)
    ]


def gradient_sum(place, grad_ref, blocks, first):
    total = None
    for i, block in enumerate(blocks):
        part = jnp.dot(grad_ref[place[first + i]], block[...], preferred_element_type=jnp.float32)
        total = part if total is None else total + part
    return total


def early_kernel(count, tokens_all, place, grad_ref, *refs):
    master_ref, out_ref = refs[count:]
    total = gradient_sum(place, grad_ref, refs[:count], 0)
    out_ref[...] = master_ref[...] - learn_rate * (total / tokens_all)


def final_kernel(first, tokens_all, place, grad_ref, block, master_ref, bits_ref, new_master_ref, new_weight_ref):
    total = gradient_sum(place, grad_ref, [block], first)
    new_master = master_ref[...] - learn_rate * (total / tokens_all)
    new_master_ref[...] = new_master
    dither = (bits_ref[...].astype(jnp.float32) + 0.5) / 16384.0
    new_weight_ref[...] = (
        new_master + (dither - 0.5) * jnp.abs(new_master) * dither_scale
    ).astype(jnp.bfloat16)


def update(place, grads, blocks, master, bits, first, tokens_all):
    rows, columns = master.shape
    depth = blocks[0].shape[0]
    tile = 256 if columns % 256 == 0 else 128
    whole = pl.BlockSpec(grads.shape, lambda j, place: (0, 0, 0))
    wide = pl.BlockSpec((rows, tile), lambda j, place: (0, j))
    block = pl.BlockSpec((depth, tile), lambda j, place: (0, j))
    last = bits is not None
    new_master = jax.ShapeDtypeStruct(master.shape, jnp.float32)
    new_weight = jax.ShapeDtypeStruct(master.shape, jnp.bfloat16)
    return pl.pallas_call(
        functools.partial(final_kernel, first, tokens_all)
        if last
        else functools.partial(early_kernel, len(blocks), tokens_all),
        grid_spec=pltpu.PrefetchScalarGridSpec(
            num_scalar_prefetch=1,
            grid=(columns // tile,),
            in_specs=[whole] + [block] * len(blocks) + [wide] * (2 if last else 1),
            out_specs=[wide, wide] if last else wide,
        ),
        out_shape=[new_master, new_weight] if last else new_master,
        compiler_params=pltpu.CompilerParams(vmem_limit_bytes=40 * 2**20),
        cost_estimate=pl.CostEstimate(
            flops=2 * rows * columns * depth * len(blocks),
            bytes_accessed=rows * columns * (14 if last else 8) + len(blocks) * depth * columns * 2,
            transcendentals=0,
        ),
    )(place, grads, *blocks, master, *([bits] if last else []))


def local(gate_act, up_act, out_grad, down_weight, master_weight, round_bits):
    n = lax.axis_size("dp")
    t = lax.axis_size("tensor")
    lines = n // 2
    me = lax.axis_index("dp")
    z, y = me // 2, me % 2
    order = arrivals(lines)
    came = {}

    def hop(rising, falling, step):
        rising = lax.ppermute(
            rising, "dp", [(2 * i + j, 2 * i + 2 + j) for i in range(step - 1, lines - 1) for j in range(2)]
        )
        falling = lax.ppermute(
            falling, "dp", [(2 * i + j, 2 * i - 2 + j) for i in range(1, lines - step + 1) for j in range(2)]
        )
        return rising, falling

    def arrived(k):
        block = None
        for key in sorted({order[i][k] for i in range(lines)}):
            here = functools.reduce(jnp.logical_or, [z == i for i in range(lines) if order[i][k] == key])
            block = came[key] if block is None else jnp.where(here, came[key], block)
        return block

    def swap(block):
        return lax.ppermute(block, "dp", [(2 * i + j, 2 * i + 1 - j) for i in range(lines) for j in range(2)])

    g = gate_act.astype(jnp.float32)
    u = up_act.astype(jnp.float32)
    sig = jax.nn.sigmoid(g)
    act = g * sig
    hidden = (act * u).astype(jnp.bfloat16)
    grad_full = lax.all_gather(out_grad, "tensor", axis=0, tiled=True)
    rising, falling = hop(hidden, hidden, 1)
    cross = [swap(hidden)]
    hidden, out_grad = lax.optimization_barrier((hidden, out_grad))
    own_cols = lax.all_to_all(out_grad, "dp", split_axis=1, concat_axis=0, tiled=True)
    partial = lax.dot_general(
        hidden, down_weight, (((1,), (1,)), ((), ())), preferred_element_type=jnp.float32
    )
    rising, falling, cross[0], partial, grad_full, own_cols = lax.optimization_barrier(
        (rising, falling, cross[0], partial, grad_full, own_cols)
    )
    layer_out = lax.psum_scatter(partial, "tensor", scatter_dimension=0, tiled=True).astype(jnp.bfloat16)
    hidden_grad = jnp.dot(grad_full, down_weight, preferred_element_type=jnp.float32)
    up_grad = (hidden_grad * act).astype(jnp.bfloat16)
    gate_grad = (hidden_grad * u * sig * (1.0 + g * (1.0 - sig))).astype(jnp.bfloat16)
    along = []
    for step in range(1, lines):
        came[1, step], came[-1, step] = rising, falling
        if step < lines - 1:
            rising, falling = hop(rising, falling, step + 1)
        along.append(arrived(step - 1))
        cross.append(swap(along[-1]))
        if step == 1:
            rising, falling, cross[1], up_grad, gate_grad = lax.optimization_barrier(
                (rising, falling, cross[1], up_grad, gate_grad)
            )
            cols = lax.all_gather(own_cols, "tensor", axis=0, tiled=False)
            rows = cols.shape[-1]
            grads = cols.reshape(t, n, out_grad.shape[0], rows).transpose(1, 3, 0, 2).reshape(n, rows, -1)
        elif step == lines - 2:
            rising, falling, cross[step], grads = lax.optimization_barrier(
                (rising, falling, cross[step], grads)
            )
        elif step < lines - 1:
            rising, falling, cross[step] = lax.optimization_barrier((rising, falling, cross[step]))
    owner = [z]
    for k in range(lines - 1):
        shift = sum(jnp.where(z == i, order[i][k][0] * order[i][k][1], 0) for i in range(lines))
        owner.append(z - shift)
    place = jnp.stack([2 * o + y for o in owner] + [2 * o + 1 - y for o in owner]).astype(jnp.int32)
    tokens_all = hidden.shape[0] * n
    master = update(place, grads, [hidden] + along + cross[:-1], master_weight, None, 0, tokens_all)
    new_master, new_weight = update(place, grads, cross[-1:], master, round_bits, n - 1, tokens_all)
    return (layer_out, gate_grad, up_grad, new_master, new_weight)


def solution(mesh):
    return jax.shard_map(
        local,
        mesh=mesh,
        in_specs=(
            P("dp", "tensor"),
            P("dp", "tensor"),
            P(("dp", "tensor"), None),
            P(None, "tensor"),
            P("dp", "tensor"),
            P("dp", "tensor"),
        ),
        out_specs=(
            P(("dp", "tensor"), None),
            P("dp", "tensor"),
            P("dp", "tensor"),
            P("dp", "tensor"),
            P("dp", "tensor"),
        ),
        check_vma=False,
    )
```

```python
import functools

import jax
import jax.numpy as jnp
from jax import lax
from jax.experimental import pallas as pl
from jax.experimental.pallas import tpu as pltpu
from jax.sharding import PartitionSpec as P

learn_rate = 0.5
dither_scale = 1.0 / 64.0


def arrivals(lines):
    return [
        [
            (way, hops)
            for hops in range(1, lines)
            for way, good in ((1, z >= hops), (-1, z + hops < lines))
            if good
        ]
        for z in range(lines)
    ]


def gradient_sum(place, grad_ref, blocks, first):
    total = None
    for i, block in enumerate(blocks):
        part = jnp.dot(grad_ref[place[first + i]], block[...], preferred_element_type=jnp.float32)
        total = part if total is None else total + part
    return total


def early_kernel(count, tokens_all, place, grad_ref, *refs):
    master_ref, out_ref = refs[count:]
    total = gradient_sum(place, grad_ref, refs[:count], 0)
    out_ref[...] = master_ref[...] - learn_rate * (total / tokens_all)


def final_kernel(first, tokens_all, place, grad_ref, block, master_ref, bits_ref, new_master_ref, new_weight_ref):
    total = gradient_sum(place, grad_ref, [block], first)
    new_master = master_ref[...] - learn_rate * (total / tokens_all)
    new_master_ref[...] = new_master
    dither = (bits_ref[...].astype(jnp.float32) + 0.5) / 16384.0
    new_weight_ref[...] = (
        new_master + (dither - 0.5) * jnp.abs(new_master) * dither_scale
    ).astype(jnp.bfloat16)


def update(place, grads, blocks, master, bits, first, tokens_all):
    rows, columns = master.shape
    depth = blocks[0].shape[0]
    tile = 256 if columns % 256 == 0 else 128
    whole = pl.BlockSpec(grads.shape, lambda j, place: (0, 0, 0))
    wide = pl.BlockSpec((rows, tile), lambda j, place: (0, j))
    block = pl.BlockSpec((depth, tile), lambda j, place: (0, j))
    last = bits is not None
    new_master = jax.ShapeDtypeStruct(master.shape, jnp.float32)
    new_weight = jax.ShapeDtypeStruct(master.shape, jnp.bfloat16)
    return pl.pallas_call(
        functools.partial(final_kernel, first, tokens_all)
        if last
        else functools.partial(early_kernel, len(blocks), tokens_all),
        grid_spec=pltpu.PrefetchScalarGridSpec(
            num_scalar_prefetch=1,
            grid=(columns // tile,),
            in_specs=[whole] + [block] * len(blocks) + [wide] * (2 if last else 1),
            out_specs=[wide, wide] if last else wide,
        ),
        out_shape=[new_master, new_weight] if last else new_master,
        compiler_params=pltpu.CompilerParams(vmem_limit_bytes=40 * 2**20),
        cost_estimate=pl.CostEstimate(
            flops=2 * rows * columns * depth * len(blocks),
            bytes_accessed=rows * columns * (14 if last else 8) + len(blocks) * depth * columns * 2,
            transcendentals=0,
        ),
    )(place, grads, *blocks, master, *([bits] if last else []))


def local(gate_act, up_act, out_grad, down_weight, master_weight, round_bits):
    n = lax.axis_size("dp")
    t = lax.axis_size("tensor")
    lines = n // 2
    me = lax.axis_index("dp")
    z, y = me // 2, me % 2
    order = arrivals(lines)
    came = {}

    def hop(rising, falling, step):
        rising = lax.ppermute(
            rising, "dp", [(2 * i + j, 2 * i + 2 + j) for i in range(step - 1, lines - 1) for j in range(2)]
        )
        falling = lax.ppermute(
            falling, "dp", [(2 * i + j, 2 * i - 2 + j) for i in range(1, lines - step + 1) for j in range(2)]
        )
        return rising, falling

    def arrived(k):
        block = None
        for key in sorted({order[i][k] for i in range(lines)}):
            here = functools.reduce(jnp.logical_or, [z == i for i in range(lines) if order[i][k] == key])
            block = came[key] if block is None else jnp.where(here, came[key], block)
        return block

    def swap(block):
        return lax.ppermute(block, "dp", [(2 * i + j, 2 * i + 1 - j) for i in range(lines) for j in range(2)])

    g = gate_act.astype(jnp.float32)
    u = up_act.astype(jnp.float32)
    sig = jax.nn.sigmoid(g)
    act = g * sig
    hidden = (act * u).astype(jnp.bfloat16)
    grad_full = lax.all_gather(out_grad, "tensor", axis=0, tiled=True)
    rising, falling = hop(hidden, hidden, 1)
    cross = [swap(hidden)]
    partial = lax.dot_general(
        hidden, down_weight, (((1,), (1,)), ((), ())), preferred_element_type=jnp.float32
    )
    rising, falling, cross[0], partial, grad_full, out_grad = lax.optimization_barrier(
        (rising, falling, cross[0], partial, grad_full, out_grad)
    )
    layer_out = lax.psum_scatter(partial, "tensor", scatter_dimension=0, tiled=True).astype(jnp.bfloat16)
    own_cols = lax.all_to_all(out_grad, "dp", split_axis=1, concat_axis=0, tiled=True)
    hidden_grad = jnp.dot(grad_full, down_weight, preferred_element_type=jnp.float32)
    up_grad = (hidden_grad * act).astype(jnp.bfloat16)
    gate_grad = (hidden_grad * u * sig * (1.0 + g * (1.0 - sig))).astype(jnp.bfloat16)
    along = []
    for step in range(1, lines):
        came[1, step], came[-1, step] = rising, falling
        if step < lines - 1:
            rising, falling = hop(rising, falling, step + 1)
        along.append(arrived(step - 1))
        cross.append(swap(along[-1]))
        if step == 1:
            rising, falling, cross[1], up_grad, gate_grad, own_cols, layer_out = lax.optimization_barrier(
                (rising, falling, cross[1], up_grad, gate_grad, own_cols, layer_out)
            )
            cols = lax.all_gather(own_cols, "tensor", axis=0, tiled=False)
            rows = cols.shape[-1]
            grads = cols.reshape(t, n, out_grad.shape[0], rows).transpose(1, 3, 0, 2).reshape(n, rows, -1)
        elif step == lines - 2:
            rising, falling, cross[step], grads = lax.optimization_barrier(
                (rising, falling, cross[step], grads)
            )
        elif step < lines - 1:
            rising, falling, cross[step] = lax.optimization_barrier((rising, falling, cross[step]))
    owner = [z]
    for k in range(lines - 1):
        shift = sum(jnp.where(z == i, order[i][k][0] * order[i][k][1], 0) for i in range(lines))
        owner.append(z - shift)
    place = jnp.stack([2 * o + y for o in owner] + [2 * o + 1 - y for o in owner]).astype(jnp.int32)
    tokens_all = hidden.shape[0] * n
    master = update(place, grads, [hidden] + along + cross[:-1], master_weight, None, 0, tokens_all)
    new_master, new_weight = update(place, grads, cross[-1:], master, round_bits, n - 1, tokens_all)
    return (layer_out, gate_grad, up_grad, new_master, new_weight)


def solution(mesh):
    return jax.shard_map(
        local,
        mesh=mesh,
        in_specs=(
            P("dp", "tensor"),
            P("dp", "tensor"),
            P(("dp", "tensor"), None),
            P(None, "tensor"),
            P("dp", "tensor"),
            P("dp", "tensor"),
        ),
        out_specs=(
            P(("dp", "tensor"), None),
            P("dp", "tensor"),
            P("dp", "tensor"),
            P("dp", "tensor"),
            P("dp", "tensor"),
        ),
        check_vma=False,
    )
```
